256 devices in a mesh: row: 8 (over x, z_hi), col: 32 (over y, z_lo, core).
Axes of the slice: x: 4, y: 4, z: 8 (z_hi: 2, z_lo: 4; z = z_hi * 4 + z_lo), core: 2. Of those that a mesh axis runs over, the one named last changes fastest.
Arguments:
- activations: bfloat16 [512, 8192], P('col', 'row'), may hold values from -22 to 22
- out_grad: bfloat16 [512, 8192], P('col', 'row'), may hold values from -2 to 2
- norm_gain: float32 [8192], P('row'), may hold values from 0.5 to 1.5
- gate_weight: bfloat16 [8192, 28672], P('row', 'col'), may hold values from -0.0625 to 0.0625
- up_weight: bfloat16 [8192, 28672], P('row', 'col'), may hold values from -0.0625 to 0.0625
- down_weight: bfloat16 [28672, 8192], P('col', 'row'), may hold values from -0.03125 to 0.03125
Outputs:
- grad_input: bfloat16 [512, 8192], P('col', 'row')
- grad_gain: float32 [8192], P('row')
- grad_gate: bfloat16 [8192, 28672], P('row', 'col')
- grad_up: bfloat16 [8192, 28672], P('row', 'col')
- grad_down: bfloat16 [28672, 8192], P('col', 'row')
The draws below stay inside these ranges and needn't reach their ends.
All inputs are finite; a program needn't handle non-finite values.
Results may differ from the reference program's by a relative error of at most 0.0067.
Values may be sent and summed in bfloat16 or wider, within the bound.
No kernel may reach another device: no remote copies, remote signals or barrier semaphores. Data moves between devices by JAX's collectives and lax.ppermute only.
A program may use at most 64 MiB of HBM per device.

```python
import jax
import jax.numpy as jnp
from jax import lax

D = 8192
FF = 28672
TOKENS = 512


def draw_activations(key, part):
    key = jax.random.fold_in(key, 11)
    first, second = jax.random.split(key, 2)
    column_scale = 0.6 * 3.0 ** (jnp.arange(D, dtype=jnp.float32) / D)
    row_scale = jnp.exp(jax.random.uniform(second, (TOKENS, 1), jnp.float32, jnp.log(0.3), jnp.log(3.0)))
    base = jax.random.normal(first, (TOKENS, D), jnp.float32)
    base = jnp.clip(base, -4.0, 4.0)
    return (base * row_scale * column_scale).astype(jnp.bfloat16)


def draw_out_grad(key, part):
    key = jax.random.fold_in(key, 23)
    first = jax.random.fold_in(key, 0)
    token_scale = 0.15 * (1.0 + 2.0 * jnp.arange(TOKENS, dtype=jnp.float32)[:, None] / TOKENS)
    base = jax.random.normal(first, (TOKENS, D), jnp.float32)
    base = jnp.clip(base, -4.0, 4.0)
    return (base * token_scale).astype(jnp.bfloat16)


def shard_levels(own_key, dims, shards, least, largest):
    factor_of, own = 1.0, jax.random.fold_in(own_key, 6)
    for axis_at, parts in shards:
        heights = jnp.exp(jax.random.uniform(jax.random.fold_in(own, axis_at), (parts,), jnp.float32, least / len(shards), largest / len(shards)))
        factor_of = factor_of * jnp.repeat(heights, dims[axis_at] // parts).reshape([-1 if axis == axis_at else 1 for axis in range(len(dims))])
    return factor_of


def gaussian(own_key, extent, deviation, limit, cuts=(), kind=jnp.bfloat16):
    values = jax.random.normal(own_key, extent, jnp.float32) * deviation
    if len(cuts) > 0:
        values = shard_levels(own_key, extent, cuts, -0.22, 0.18) * values
    return jnp.clip(values, min=-limit, max=limit).astype(kind)


def setup_inputs(seed: int = 0) -> dict:
    splits = jax.random.split(jax.random.key(seed), 7)
    activations = draw_activations(jax.random.fold_in(splits[6], 71), 0)
    out_grad = draw_out_grad(jax.random.fold_in(splits[6], 71), 0)
    norm_gain = jnp.clip(1.0 + 0.1 * jax.random.normal(splits[2], (D,), jnp.float32), 0.5, 1.5)
    gate_weight = gaussian(splits[3], (D, FF), D ** -0.5, 0.0625, ((0, 8), (1, 32)))
    up_weight = gaussian(splits[4], (D, FF), D ** -0.5, 0.0625, ((0, 8), (1, 32)))
    down_weight = gaussian(splits[5], (FF, D), FF ** -0.5, 0.03125, ((0, 32), (1, 8)))
    return dict(activations=activations, out_grad=out_grad, norm_gain=norm_gain, gate_weight=gate_weight, up_weight=up_weight, down_weight=down_weight)


def swiglu_grads(gate, up, back):
    sig = jax.nn.sigmoid(gate)
    silu = gate * sig
    d_gate = back * up * sig * (1.0 + gate * (1.0 - sig))
    d_up = back * silu
    hidden = silu * up
    return (d_gate.astype(jnp.bfloat16), d_up.astype(jnp.bfloat16), hidden.astype(jnp.bfloat16))

def reference(activations, out_grad, norm_gain, gate_weight, up_weight, down_weight):
    x_full = activations.astype(jnp.float32)
    inv_rms = lax.rsqrt(lax.optimization_barrier(jnp.sum(x_full * x_full, axis=1, keepdims=True)) / D + 1e-05)
    normed = (x_full * inv_rms * norm_gain).astype(jnp.bfloat16)
    gate = jnp.dot(normed, gate_weight, preferred_element_type=jnp.float32)
    up = jnp.dot(normed, up_weight, preferred_element_type=jnp.float32)
    back = jnp.dot(out_grad, down_weight.T, preferred_element_type=jnp.float32)
    d_gate, d_up, hidden = swiglu_grads(gate, up, back)
    grad_gate = jnp.dot(normed.T, d_gate, preferred_element_type=jnp.float32).astype(jnp.bfloat16)
    grad_up = jnp.dot(normed.T, d_up, preferred_element_type=jnp.float32).astype(jnp.bfloat16)
    grad_down = jnp.dot(hidden.T, out_grad, preferred_element_type=jnp.float32).astype(jnp.bfloat16)
    grad_normed = jnp.dot(d_gate, gate_weight.T, preferred_element_type=jnp.float32) + jnp.dot(d_up, up_weight.T, preferred_element_type=jnp.float32)
    grad_gain = lax.optimization_barrier(jnp.sum(grad_normed * x_full * inv_rms, axis=0))
    scaled = grad_normed * norm_gain
    mean_term = lax.optimization_barrier(jnp.sum(scaled * x_full, axis=1, keepdims=True)) / D
    grad_input = (inv_rms * scaled - x_full * inv_rms * inv_rms * inv_rms * mean_term).astype(jnp.bfloat16)
    return (grad_input, grad_gain, grad_gate, grad_up, grad_down)
```

```python
import jax
import jax.numpy as jnp
from jax import lax
from jax.experimental import pallas as pl
from jax.experimental.pallas import tpu as pltpu
from jax.sharding import Mesh
from jax.sharding import PartitionSpec as P

D = 8192
BF = jnp.bfloat16
F32 = jnp.float32
LANES = 128
AXES = ("x", "zh", "y", "zl", "core")
CONTRACT_LAST = (((1,), (1,)), ((), ()))
CONTRACT_FIRST = (((0,), (0,)), ((), ()))


def ring(size, step):
    return [(i, (i + step) % size) for i in range(size)]


def send_x(value, step):
    return lax.ppermute(value, "x", ring(4, step))


def send_y(value, step):
    return lax.ppermute(value, "y", ring(4, step))


def swap(value, axis):
    return lax.ppermute(value, axis, ring(2, 1))


def slot_pairs(slot):
    return [(x * 4 + (zl + x + slot) % 4, x * 4 + zl) for x in range(4) for zl in range(4)]


def gather_slot(value, slot):
    return lax.ppermute(value, ("x", "zl"), slot_pairs(slot))


def return_slot(value, slot):
    return lax.ppermute(value, ("x", "zl"), [(b, a) for a, b in slot_pairs(slot)])


def pieces(column):
    hi = column.astype(BF)
    rest = column - hi.astype(F32)
    mid = rest.astype(BF)
    low = (rest - mid.astype(F32)).astype(BF)
    return [hi, mid, low]


def tail(*columns):
    parts = [p.astype(F32) for c in columns for p in pieces(c)]
    lane = lax.broadcasted_iota(jnp.int32, (columns[0].shape[0], LANES), 1)
    out = jnp.zeros((columns[0].shape[0], LANES), F32)
    for i, part in enumerate(parts):
        out = jnp.where(lane == i, part, out)
    return out


def head(block, at):
    return block[:, at : at + 1] + block[:, at + 1 : at + 2] + block[:, at + 2 : at + 3]


def call(body, out_shapes, *args):
    def kernel(*refs):
        outs = body(*[r[...] for r in refs[: len(args)]])
        for ref, out in zip(refs[len(args) :], outs):
            ref[...] = out

    return pl.pallas_call(
        kernel,
        out_shape=[jax.ShapeDtypeStruct(s, d) for s, d in out_shapes],
        compiler_params=pltpu.CompilerParams(vmem_limit_bytes=48 * 1024 * 1024),
    )(*args)


def tokens(own, other, which):
    return jnp.concatenate([part[s, which] for s in range(4) for part in (own, other)], axis=0)


def forward(own, other, gain, gate_w, up_w, down_w):
    x = tokens(own, other, 0).astype(F32)
    scaled = (x * gain).astype(BF)
    grad = tokens(own, other, 1)
    square = jnp.sum(x * x, axis=1, keepdims=True)
    sums = jnp.concatenate(
        [
            jnp.dot(scaled, gate_w, preferred_element_type=F32),
            jnp.dot(scaled, up_w, preferred_element_type=F32),
            lax.dot_general(grad, down_w, CONTRACT_LAST, preferred_element_type=F32),
            tail(square),
        ],
        axis=1,
    )
    return [sums[0:32]] + [sums[32 * s : 32 * s + 32].astype(BF) for s in (1, 2, 3)]


def add_x(own, a, b, c):
    total = own + a.astype(F32) + b.astype(F32) + c.astype(F32)
    end = tail(head(total[:, -LANES:], 0))
    total = jnp.concatenate([total[:, :-LANES], end], axis=1)
    return [total, total.astype(BF)]


def activate(own, other):
    total = own + other.astype(F32)
    width = (total.shape[1] - LANES) // 3
    inv = lax.rsqrt(head(total[:, -LANES:], 0) / D + 1e-05)
    gate = total[:, :width] * inv
    up = total[:, width : 2 * width] * inv
    back = total[:, 2 * width : 3 * width]
    sig = 1.0 / (1.0 + jnp.exp(-gate))
    silu = gate * sig
    d_gate = back * up * sig * (1.0 + gate * (1.0 - sig))
    d_up = back * silu
    hidden = silu * up
    mean = jnp.sum(d_gate * gate + d_up * up, axis=1, keepdims=True)
    return [jnp.concatenate([d_gate, d_up, hidden, tail(inv, mean)], axis=1).astype(BF)]


def backward(m0, m1, m2, m3, own, other, gate_w, up_w):
    width = gate_w.shape[1]
    message = jnp.concatenate([m0, m1, m2, m3], axis=0)
    part = lax.dot_general(
        message[:, :width], gate_w, CONTRACT_LAST, preferred_element_type=F32
    ) + lax.dot_general(
        message[:, width : 2 * width], up_w, CONTRACT_LAST, preferred_element_type=F32
    )
    end = message[:, -LANES:].astype(F32)
    inv = head(end, 0)
    x = tokens(own, other, 0).astype(F32)
    gain = jnp.sum(part * x * inv, axis=0, keepdims=True)
    part = jnp.concatenate([part, tail(head(end, 3))], axis=1)
    mine = jnp.concatenate([part[32 * s : 32 * s + 16] for s in range(4)], axis=0)
    theirs = jnp.concatenate([part[32 * s + 16 : 32 * s + 32] for s in range(4)], axis=0)
    return [mine, theirs, gain, inv]


def add_core(mine, received):
    total = mine + received
    end = tail(head(total[:, -LANES:], 0))
    return [jnp.concatenate([total[:, :-LANES], end], axis=1).astype(BF)]


def weights(width, *args):
    messages, blocks, invs, gain = args[0:16], args[16:24], args[24:28], args[28]
    message = jnp.concatenate(messages, axis=0)
    normed = jnp.concatenate(
        [
            (tokens(blocks[2 * i], blocks[2 * i + 1], 0).astype(F32) * invs[i] * gain).astype(BF)
            for i in range(4)
        ],
        axis=0,
    )
    grad = jnp.concatenate([tokens(blocks[2 * i], blocks[2 * i + 1], 1) for i in range(4)], axis=0)
    first = lax.dot_general(normed, message[:, :width], CONTRACT_FIRST, preferred_element_type=F32)
    second = lax.dot_general(
        normed, message[:, width : 2 * width], CONTRACT_FIRST, preferred_element_type=F32
    )
    third = lax.dot_general(
        message[:, 2 * width : 3 * width], grad, CONTRACT_FIRST, preferred_element_type=F32
    )
    return [first.astype(BF), second.astype(BF), third.astype(BF)]


def shards(activations, out_grad, norm_gain, gate_w, up_w, down_w):
    rows, depth = activations.shape
    width = gate_w.shape[1]
    wide = 3 * width + LANES
    gain = norm_gain[None, :]

    both = jnp.stack([activations, out_grad])
    home = jnp.stack([gather_slot(both, s) for s in range(4)])
    steps = (0, 1, -1, 2)
    own = [home] + [send_y(home, s) for s in steps[1:]]
    other = [swap(o, "core") for o in own]

    messages, invs, gains, parts = [], [], [], []
    for i in range(4):
        s0, s1, s2, s3 = call(
            forward,
            [((32, wide), F32)] + [((32, wide), BF)] * 3,
            own[i], other[i], gain, gate_w, up_w, down_w,
        )
        total, out = call(
            add_x,
            [((32, wide), F32), ((32, wide), BF)],
            s0, send_x(s1, 1), send_x(s3, -1), send_x(s2, 2),
        )
        (m0,) = call(activate, [((32, wide), BF)], total, swap(out, "zh"))
        group = [m0, send_x(m0, -1), send_x(m0, 2), send_x(m0, 1)]
        mine, theirs, part_gain, inv = call(
            backward,
            [((64, depth + LANES), F32)] * 2 + [((1, depth), F32), ((128, 1), F32)],
            *group, own[i], other[i], gate_w, up_w,
        )
        (part,) = call(add_core, [((64, depth + LANES), BF)], mine, swap(theirs, "core"))
        messages += group
        invs.append(inv)
        gains.append(part_gain)
        parts.append(send_y(part, -steps[i]) if i else part)

    total = sum(p.astype(F32) for p in parts).reshape(4, rows, depth + LANES)
    total = sum(return_slot(total[s], s) for s in range(4))
    grad_normed = total[:, :depth]
    mean = head(total[:, depth:], 0)

    part_gain = sum(gains)
    part_gain = part_gain + swap(part_gain, "core")
    part_gain = sum([part_gain] + [send_y(part_gain, s) for s in (1, -1, 2)])
    part_gain = sum(
        [part_gain] + [lax.ppermute(part_gain, "zl", ring(4, s)) for s in (1, 2, 3)]
    )

    x_full = activations.astype(F32)
    slot = lax.rem(8 - lax.axis_index("x"), 4)
    inv = lax.dynamic_slice(invs[0], (slot * 32, 0), (rows, 1))
    grad_input = inv * grad_normed * gain - x_full * inv * inv * (mean / D)

    grad_gate, grad_up, grad_down = call(
        lambda *a: weights(width, *a),
        [((depth, width), BF), ((depth, width), BF), ((width, depth), BF)],
        *messages, *[v for pair in zip(own, other) for v in pair], *invs, gain,
    )
    return (grad_input.astype(BF), part_gain[0], grad_gate, grad_up, grad_down)


def solution(mesh):
    fine = Mesh(mesh.devices.reshape(4, 2, 4, 4, 2), AXES)
    row, col = ("x", "zh"), ("y", "zl", "core")
    in_specs = (P(col, row), P(col, row), P(row), P(row, col), P(row, col), P(col, row))
    out_specs = (P(col, row), P(row), P(row, col), P(row, col), P(col, row))
    return jax.shard_map(shards, mesh=fine, in_specs=in_specs, out_specs=out_specs, check_vma=False)
```

```python
import jax
import jax.numpy as jnp
from jax import lax
from jax.experimental import pallas as pl
from jax.experimental.pallas import tpu as pltpu
from jax.sharding import Mesh
from jax.sharding import PartitionSpec as P

D = 8192
BF = jnp.bfloat16
F32 = jnp.float32
LANES = 128
AXES = ("x", "zh", "y", "zl", "core")
CONTRACT_LAST = (((1,), (1,)), ((), ()))
CONTRACT_FIRST = (((0,), (0,)), ((), ()))
STEPS = (0, 1, -1, 2)
PARTS = 4
EXTRA = 16
GROUPS = ((0, 1), (2, 3))
GAINS = GROUPS[-1]


def ring(size, step):
    return [(i, (i + step) % size) for i in range(size)]


def send(value, axis, step):
    return lax.ppermute(value, axis, ring(2 if axis in ("zh", "core") else 4, step))


def tail(*columns):
    lane = lax.broadcasted_iota(jnp.int32, (columns[0].shape[0], LANES), 1)
    out = jnp.zeros((columns[0].shape[0], LANES), F32)
    at = 0
    for rest in columns:
        for _ in range(3):
            piece = rest.astype(BF).astype(F32)
            out = jnp.where(lane == at, piece, out)
            rest = rest - piece
            at += 1
    return out


def head(block, at):
    return block[:, at : at + 1] + block[:, at + 1 : at + 2] + block[:, at + 2 : at + 3]


def call(kernel, out_shapes, args, limit=24, flops=0):
    return pl.pallas_call(
        kernel,
        out_shape=[jax.ShapeDtypeStruct(s, d) for s, d in out_shapes],
        compiler_params=pltpu.CompilerParams(vmem_limit_bytes=limit * 1024 * 1024),
    )(*args)


def load(weights):
    count = len(weights)

    def kernel(*refs):
        sems, copies = refs[-1], []
        for n, (source, target) in enumerate(zip(refs[:count], refs[count : 2 * count])):
            step = source.shape[0] // PARTS
            for p in range(PARTS):
                rows = pl.ds(p * step, step)
                copies.append(
                    pltpu.make_async_copy(source.at[rows], target.at[rows], sems.at[n, p])
                )
        for copy in copies:
            copy.start()
        for copy in copies:
            copy.wait()

    return pl.pallas_call(
        kernel,
        out_shape=[jax.ShapeDtypeStruct(w.shape, w.dtype) for w in weights],
        in_specs=[pl.BlockSpec(memory_space=pltpu.HBM)] * count,
        out_specs=[pl.BlockSpec(memory_space=pltpu.VMEM)] * count,
        scratch_shapes=[pltpu.SemaphoreType.DMA((count, PARTS))],
        compiler_params=pltpu.CompilerParams(vmem_limit_bytes=24 * 1024 * 1024),
    )(*[pltpu.with_memory_space_constraint(w, pltpu.HBM) for w in weights])


def split(row):
    line = lax.broadcasted_iota(jnp.int32, (EXTRA, row.shape[1]), 0)
    out = jnp.zeros((EXTRA, row.shape[1]), F32)
    for at in range(3):
        piece = row.astype(BF).astype(F32)
        out = jnp.where(line == at, piece, out)
        row = row - piece
    return out.astype(BF)


def joined(block):
    block = block.astype(F32)
    return block[0:1] + block[1:2] + block[2:3]


def label(slot):
    return lax.rem(lax.axis_index("x") + slot, 4)


def tokens(blocks, which):
    at = [label(s) for s in range(4)]
    return jnp.concatenate(
        [ref[at[s], which] for s in range(4) for pair in blocks for ref in pair], axis=0
    )


def pairs(refs):
    return [(refs[i], refs[i + 1]) for i in range(0, len(refs), 2)]


def forward(size, *refs):
    blocks, (gain, gate_w, up_w, down_w, *outs) = pairs(refs[: 2 * size]), refs[2 * size :]
    x = tokens(blocks, 0).astype(F32)
    scaled = (x * gain[...]).astype(BF)
    grad = tokens(blocks, 1)
    rows, width = 32 * size, gate_w.shape[1]

    def put(value, start):
        for s in range(4):
            part = value[rows * s : rows * s + rows]
            outs[s][:, start : start + value.shape[1]] = part.astype(outs[s].dtype)

    put(jnp.dot(scaled, gate_w[...], preferred_element_type=F32), 0)
    put(jnp.dot(scaled, up_w[...], preferred_element_type=F32), width)
    put(
        lax.dot_general(grad, down_w[...], CONTRACT_LAST, preferred_element_type=F32),
        2 * width,
    )
    put(tail(jnp.sum(x * x, axis=1, keepdims=True)), 3 * width)


def add_x(own, a, b, c, total, out):
    value = own[...] + a[...].astype(F32) + b[...].astype(F32) + c[...].astype(F32)
    end = tail(head(value[:, -LANES:], 0))
    value = jnp.concatenate([value[:, :-LANES], end], axis=1)
    total[...] = value
    out[...] = value.astype(BF)


def activate(own, other, out):
    total = own[...] + other[...].astype(F32)
    width = (total.shape[1] - LANES) // 3
    inv = lax.rsqrt(head(total[:, -LANES:], 0) / D + 1e-05)
    gate = total[:, :width] * inv
    up = total[:, width : 2 * width] * inv
    back = total[:, 2 * width : 3 * width]
    sig = 1.0 / (1.0 + jnp.exp(-gate))
    silu = gate * sig
    d_gate = back * up * sig * (1.0 + gate * (1.0 - sig))
    d_up = back * silu
    mean = jnp.sum(d_gate * gate + d_up * up, axis=1, keepdims=True)
    out[:, :width] = d_gate.astype(BF)
    out[:, width : 2 * width] = d_up.astype(BF)
    out[:, 2 * width : 3 * width] = (silu * up).astype(BF)
    out[:, 3 * width :] = tail(inv, mean).astype(BF)


def backward(size, *refs):
    messages, blocks = refs[:4], pairs(refs[4 : 4 + 2 * size])
    gate_w, up_w, last_gain, mine, theirs, inv_out, gain_out = refs[4 + 2 * size :]
    rows, (depth, width) = 32 * size, gate_w.shape

    def rows_of(start, stop):
        return jnp.concatenate([m[:, start:stop] for m in messages], axis=0)

    part = lax.dot_general(
        rows_of(0, width), gate_w[...], CONTRACT_LAST, preferred_element_type=F32
    ) + lax.dot_general(
        rows_of(width, 2 * width), up_w[...], CONTRACT_LAST, preferred_element_type=F32
    )
    end = rows_of(3 * width, 3 * width + LANES).astype(F32)
    inv = head(end, 0)
    mean = tail(head(end, 3))
    x = tokens(blocks, 0).astype(F32)
    gain = last_gain[...] + jnp.sum(part * x * inv, axis=0, keepdims=True)
    for s in range(4):
        at = label(s)
        inv_out[at] = inv[rows * s : rows * s + rows]
        for i in range(size):
            place = pl.ds(pl.multiple_of(64 * i + 16 * at, 16), 16)
            for core, out in enumerate((mine, theirs)):
                start = rows * s + 32 * i + 16 * core
                out[place, :depth] = part[start : start + 16]
                out[place, depth:] = mean[start : start + 16]
    gain_out[...] = gain
    theirs[64 * size :, :depth] = jnp.broadcast_to(gain, (8, depth))
    theirs[64 * size :, depth:] = jnp.zeros((8, LANES), F32)


def add_core(*refs):
    count = len(GROUPS)
    mine, received, gains, outs = refs[:count], refs[count : 2 * count], refs[-5], refs[-4:]
    depth = gains.shape[1]
    last = 64 * len(GROUPS[-1])
    gain = gains[...] + received[-1][last : last + 1, :depth]
    for g, group in enumerate(GROUPS):
        for i, block in enumerate(group):
            rows = slice(64 * i, 64 * i + 64)
            value, out = mine[g][rows] + received[g][rows], outs[block]
            out[:64, :depth] = value[:, :depth].astype(BF)
            out[:64, depth:] = tail(head(value[:, depth:], 0)).astype(BF)
            out[64:, :depth] = split(gain)
            out[64:, depth:] = jnp.zeros((EXTRA, LANES), BF)


def add_y(*refs):
    parts, outs = refs[:4], refs[4:]
    depth = parts[0].shape[1] - LANES
    total = sum(p[:64].astype(F32) for p in parts)
    gain = sum(joined(p[64:, :depth]) for p in parts)
    outs[0][:16] = total[:16]
    outs[0][16:, :depth] = jnp.broadcast_to(gain, (EXTRA, depth))
    outs[0][16:, depth:] = jnp.zeros((EXTRA, LANES), F32)
    for s in range(1, 4):
        outs[s][:16, :depth] = total[16 * s : 16 * s + 16, :depth].astype(BF)
        outs[s][:16, depth:] = tail(head(total[16 * s : 16 * s + 16, depth:], 0)).astype(BF)
        outs[s][16:, :depth] = split(gain)
        outs[s][16:, depth:] = jnp.zeros((EXTRA, LANES), BF)


def finish(own, a, b, c, x, inv, gain, grad_input, grad_gain):
    depth = x.shape[1]
    total = own[:16] + sum(v[:16].astype(F32) for v in (a, b, c))
    inv = inv[0, :16]
    mean = head(total[:, depth:], 0) / D
    grad_gain[...] = own[16:17, :depth] + sum(joined(v[16:, :depth]) for v in (a, b, c))
    grad_input[...] = (
        inv * total[:, :depth] * gain[...] - x[...].astype(F32) * inv * inv * mean
    ).astype(BF)


def wide_grads(at, *refs):
    count = len(GROUPS)
    messages, blocks = refs[: 4 * count], pairs(refs[4 * count : 4 * count + 8])
    invs, (gain, out) = refs[4 * count + 8 : -2], refs[-2:]
    width = out.shape[1]
    normed = []
    for g, group in enumerate(GROUPS):
        members = [blocks[i] for i in group]
        inv = jnp.concatenate([invs[g][label(s)] for s in range(4)], axis=0)
        normed.append((tokens(members, 0).astype(F32) * inv * gain[...]).astype(BF))
    columns = jnp.concatenate([m[:, at * width : at * width + width] for m in messages], axis=0)
    out[...] = lax.dot_general(
        jnp.concatenate(normed, axis=0), columns, CONTRACT_FIRST, preferred_element_type=F32
    ).astype(BF)


def down_grads(*refs):
    count = len(GROUPS)
    messages, blocks, out = refs[: 4 * count], pairs(refs[4 * count : -1]), refs[-1]
    width = out.shape[0]
    grads = jnp.concatenate([tokens([blocks[i] for i in g], 1) for g in GROUPS], axis=0)
    hidden = jnp.concatenate([m[:, 2 * width : 3 * width] for m in messages], axis=0)
    out[...] = lax.dot_general(
        hidden, grads, CONTRACT_FIRST, preferred_element_type=F32
    ).astype(BF)


def after(value, *earlier):
    return lax.optimization_barrier((value, *earlier))[0]


def shards(activations, out_grad, norm_gain, gate_w, up_w, down_w):
    rows, depth = activations.shape
    width = gate_w.shape[1]
    wide, deep = 3 * width + LANES, depth + LANES
    gain = norm_gain[None, :]

    gate_w, up_w, down_w = load([gate_w, up_w, down_w])
    both = jnp.stack([activations, out_grad])
    home = jnp.stack([both] + [send(both, "zl", -k) for k in (1, 2, 3)])
    own = [home] + [send(home, "y", s) for s in STEPS[1:]]
    own[1] = after(own[1], gate_w, up_w, down_w)
    other = [send(o, "core", 1) for o in own]

    def members(group):
        return [v for i in group for v in (own[i], other[i])]

    unit = 2 * depth * width * 128
    totals, crossed = [], []
    for group in GROUPS:
        tall = 32 * len(group)
        s0, s1, s2, s3 = call(
            lambda *a, n=len(group): forward(n, *a),
            [((tall, wide), F32)] + [((tall, wide), BF)] * 3,
            [*members(group), gain, gate_w, up_w, down_w],
            flops=3 * unit * len(group),
        )
        total, out = call(
            add_x,
            [((tall, wide), F32), ((tall, wide), BF)],
            [s0, send(s1, "x", 1), send(s2, "x", 2), send(s3, "x", -1)],
        )
        totals.append(total)
        crossed.append(send(out, "zh", 1))

    messages, invs, halves = [], [], []
    gains = jnp.zeros((1, depth), F32)
    for group, total, arrived in zip(GROUPS, totals, crossed):
        size = len(group)
        tall = 32 * size
        (m0,) = call(activate, [((tall, wide), BF)], [total, arrived])
        found = [m0, send(m0, "x", -1), send(m0, "x", 2), send(m0, "x", 1)]
        mine, theirs, inv, gains = call(
            lambda *a, n=size: backward(n, *a),
            [((64 * size, deep), F32), ((64 * size + 8, deep), F32), ((4, tall, 1), F32)]
            + [((1, depth), F32)],
            [*found, *members(group), gate_w, up_w, gains],
            flops=2 * unit * size,
        )
        halves.append((mine, send(theirs, "core", 1)))
        messages += found
        invs.append(inv)

    parts = call(
        add_core,
        [((64 + EXTRA, deep), BF)] * 4,
        [*[h[0] for h in halves], *[h[1] for h in halves], gains],
    )
    parts = [parts[0]] + [send(parts[i], "y", -STEPS[i]) for i in (1, 2, 3)]
    outs = call(
        add_y, [((16 + EXTRA, deep), F32)] + [((16 + EXTRA, deep), BF)] * 3, parts
    )
    flat = [v for pair in zip(own, other) for v in pair]
    (grad_down,) = call(
        down_grads, [((width, depth), BF)], [*messages, *flat], limit=32, flops=4 * unit
    )
    grad_gate, grad_up = (
        call(
            lambda *a, n=at: wide_grads(n, *a),
            [((depth, width), BF)],
            [*messages, *flat, *invs, gain],
            limit=32,
            flops=4 * unit,
        )[0]
        for at in (0, 1)
    )
    home_sums = [outs[0]]
    home_sums += [send(after(outs[k], grad_down, grad_up), "zl", k) for k in (1, 2, 3)]
    grad_input, grad_gain = call(
        finish,
        [((rows, depth), BF), ((1, depth), F32)],
        [*home_sums, activations, invs[0], gain],
    )
    return (grad_input, grad_gain[0], grad_gate, grad_up, grad_down)


def solution(mesh):
    fine = Mesh(mesh.devices.reshape(4, 2, 4, 4, 2), AXES)
    row, col = ("x", "zh"), ("y", "zl", "core")
    in_specs = (P(col, row), P(col, row), P(row), P(row, col), P(row, col), P(col, row))
    out_specs = (P(col, row), P(row), P(row, col), P(row, col), P(col, row))
    return jax.shard_map(shards, mesh=fine, in_specs=in_specs, out_specs=out_specs, check_vma=False)
```

```python
import jax
import jax.numpy as jnp
from jax import lax
from jax.experimental import pallas as pl
from jax.experimental.pallas import tpu as pltpu
from jax.sharding import Mesh
from jax.sharding import PartitionSpec as P

D = 8192
BF = jnp.bfloat16
F32 = jnp.float32
LANES = 128
AXES = ("x", "zh", "y", "zl", "core")
CONTRACT_LAST = (((1,), (1,)), ((), ()))
CONTRACT_FIRST = (((0,), (0,)), ((), ()))
STEPS = (0, 1, -1, 2)
PARTS = 4
GROUPS = ((0, 1), (2, 3))
GAINS = GROUPS[-1]


def ring(size, step):
    return [(i, (i + step) % size) for i in range(size)]


def send(value, axis, step):
    return lax.ppermute(value, axis, ring(2 if axis in ("zh", "core") else 4, step))


def tail(*columns):
    lane = lax.broadcasted_iota(jnp.int32, (columns[0].shape[0], LANES), 1)
    out = jnp.zeros((columns[0].shape[0], LANES), F32)
    at = 0
    for rest in columns:
        for _ in range(3):
            piece = rest.astype(BF).astype(F32)
            out = jnp.where(lane == at, piece, out)
            rest = rest - piece
            at += 1
    return out


def head(block, at):
    return block[:, at : at + 1] + block[:, at + 1 : at + 2] + block[:, at + 2 : at + 3]


def call(kernel, out_shapes, args, limit=24):
    return pl.pallas_call(
        kernel,
        out_shape=[jax.ShapeDtypeStruct(s, d) for s, d in out_shapes],
        compiler_params=pltpu.CompilerParams(vmem_limit_bytes=limit * 1024 * 1024),
    )(*args)


def load(weights):
    count = len(weights)

    def kernel(*refs):
        sems, copies = refs[-1], []
        for n, (source, target) in enumerate(zip(refs[:count], refs[count : 2 * count])):
            step = source.shape[0] // PARTS
            for p in range(PARTS):
                rows = pl.ds(p * step, step)
                copies.append(
                    pltpu.make_async_copy(source.at[rows], target.at[rows], sems.at[n, p])
                )
        for copy in copies:
            copy.start()
        for copy in copies:
            copy.wait()

    return pl.pallas_call(
        kernel,
        out_shape=[jax.ShapeDtypeStruct(w.shape, w.dtype) for w in weights],
        in_specs=[pl.BlockSpec(memory_space=pltpu.HBM)] * count,
        out_specs=[pl.BlockSpec(memory_space=pltpu.VMEM)] * count,
        scratch_shapes=[pltpu.SemaphoreType.DMA((count, PARTS))],
        compiler_params=pltpu.CompilerParams(vmem_limit_bytes=24 * 1024 * 1024),
    )(*[pltpu.with_memory_space_constraint(w, pltpu.HBM) for w in weights])


def pack(row, rows):
    pieces = []
    for _ in range(3):
        pieces.append(row.astype(BF).astype(F32))
        row = row - pieces[-1]
    cuts = row.shape[1] // LANES
    line = lax.broadcasted_iota(jnp.int32, (rows, LANES), 0)
    tiles = [jnp.zeros((rows, LANES), F32) for _ in range(-(-3 * cuts // rows))]
    for at in range(3 * cuts):
        piece = pieces[at // cuts][:, at % cuts * LANES : at % cuts * LANES + LANES]
        tiles[at // rows] = jnp.where(line == at % rows, piece, tiles[at // rows])
    return jnp.concatenate(tiles, axis=1).astype(BF)


def unpack(block, width):
    block, rows, cuts = block.astype(F32), block.shape[0], width // LANES
    cut = [
        block[at % rows : at % rows + 1, at // rows * LANES : at // rows * LANES + LANES]
        for at in range(3 * cuts)
    ]
    return sum(jnp.concatenate(cut[p * cuts : p * cuts + cuts], axis=1) for p in range(3))


def label(slot):
    return lax.rem(lax.axis_index("x") + slot, 4)


def tokens(blocks, which):
    at = [label(s) for s in range(4)]
    return jnp.concatenate(
        [ref[at[s], which] for s in range(4) for pair in blocks for ref in pair], axis=0
    )


def pairs(refs):
    return [(refs[i], refs[i + 1]) for i in range(0, len(refs), 2)]


def forward(size, *refs):
    blocks, (gain, gate_w, up_w, down_w, *outs) = pairs(refs[: 2 * size]), refs[2 * size :]
    x = tokens(blocks, 0).astype(F32)
    scaled = (x * gain[...]).astype(BF)
    grad = tokens(blocks, 1)
    rows, width = 32 * size, gate_w.shape[1]

    def put(value, start):
        for s in range(4):
            part = value[rows * s : rows * s + rows]
            outs[s][:, start : start + value.shape[1]] = part.astype(outs[s].dtype)

    put(jnp.dot(scaled, gate_w[...], preferred_element_type=F32), 0)
    put(jnp.dot(scaled, up_w[...], preferred_element_type=F32), width)
    put(
        lax.dot_general(grad, down_w[...], CONTRACT_LAST, preferred_element_type=F32),
        2 * width,
    )
    put(tail(jnp.sum(x * x, axis=1, keepdims=True)), 3 * width)


def add_x(own, a, b, c, total, out):
    value = own[...] + a[...].astype(F32) + b[...].astype(F32) + c[...].astype(F32)
    end = tail(head(value[:, -LANES:], 0))
    value = jnp.concatenate([value[:, :-LANES], end], axis=1)
    total[...] = value
    out[...] = value.astype(BF)


def activate(own, other, out, hidden=None):
    total = own[...] + other[...].astype(F32)
    width = (total.shape[1] - LANES) // 3
    inv = lax.rsqrt(head(total[:, -LANES:], 0) / D + 1e-05)
    gate = total[:, :width] * inv
    up = total[:, width : 2 * width] * inv
    back = total[:, 2 * width : 3 * width]
    sig = 1.0 / (1.0 + jnp.exp(-gate))
    silu = gate * sig
    d_gate = back * up * sig * (1.0 + gate * (1.0 - sig))
    d_up = back * silu
    mean = jnp.sum(d_gate * gate + d_up * up, axis=1, keepdims=True)
    out[:, :width] = d_gate.astype(BF)
    out[:, width : 2 * width] = d_up.astype(BF)
    out[:, 2 * width : 2 * width + LANES] = tail(inv, mean).astype(BF)
    if hidden is None:
        out[:, 2 * width + LANES :] = (silu * up).astype(BF)
    else:
        hidden[...] = (silu * up).astype(BF)


def backward(size, *refs):
    messages, blocks = refs[:4], pairs(refs[4 : 4 + 2 * size])
    gate_w, up_w, last_gain, mine, theirs, inv_out, gain_out = refs[4 + 2 * size :]
    rows, (depth, width) = 32 * size, gate_w.shape

    def rows_of(start, stop):
        return jnp.concatenate([m[:, start:stop] for m in messages], axis=0)

    part = lax.dot_general(
        rows_of(0, width), gate_w[...], CONTRACT_LAST, preferred_element_type=F32
    ) + lax.dot_general(
        rows_of(width, 2 * width), up_w[...], CONTRACT_LAST, preferred_element_type=F32
    )
    end = rows_of(2 * width, 2 * width + LANES).astype(F32)
    inv = head(end, 0)
    mean = tail(head(end, 3))
    x = tokens(blocks, 0).astype(F32)
    gain = last_gain[...] + jnp.sum(part * x * inv, axis=0, keepdims=True)
    for s in range(4):
        at = label(s)
        inv_out[at] = inv[rows * s : rows * s + rows]
        for i in range(size):
            place = pl.ds(pl.multiple_of(64 * i + 16 * at, 16), 16)
            for core, out in enumerate((mine, theirs)):
                start = rows * s + 32 * i + 16 * core
                out[place, :depth] = part[start : start + 16]
                out[place, depth:] = mean[start : start + 16]
    gain_out[...] = gain
    theirs[64 * size :, :depth] = jnp.broadcast_to(gain, (8, depth))
    theirs[64 * size :, depth:] = jnp.zeros((8, LANES), F32)


def add_core(*refs):
    count = len(GROUPS)
    mine, received, gains, outs = refs[:count], refs[count : 2 * count], refs[-5], refs[-4:]
    depth = gains.shape[1]
    last = 64 * len(GROUPS[-1])
    packed = pack(gains[...] + received[-1][last : last + 1, :depth], 64)
    for g, group in enumerate(GROUPS):
        for i, block in enumerate(group):
            rows = slice(64 * i, 64 * i + 64)
            value, out = mine[g][rows] + received[g][rows], outs[block]
            out[:, :depth] = value[:, :depth].astype(BF)
            out[:, depth : depth + LANES] = tail(head(value[:, depth:], 0)).astype(BF)
            out[:, depth + LANES :] = packed


def add_y(*refs):
    parts, gain_out, outs = refs[:4], refs[4], refs[5:]
    depth = gain_out.shape[1]
    deep = depth + LANES
    total = sum(p[:, :deep].astype(F32) for p in parts)
    gain = sum(unpack(p[:, deep:], depth) for p in parts)
    gain_out[...] = gain
    outs[0][...] = total[:16]
    packed = pack(gain, 16)
    for s in range(1, 4):
        outs[s][:, :depth] = total[16 * s : 16 * s + 16, :depth].astype(BF)
        outs[s][:, depth:deep] = tail(head(total[16 * s : 16 * s + 16, depth:], 0)).astype(BF)
        outs[s][:, deep:] = packed


def finish(own, a, b, c, own_gain, x, inv, gain, grad_input, grad_gain):
    depth = x.shape[1]
    deep = depth + LANES
    total = own[...] + sum(v[:, :deep].astype(F32) for v in (a, b, c))
    inv = inv[0, :16]
    mean = head(total[:, depth:], 0) / D
    grad_gain[...] = own_gain[...] + sum(unpack(v[:, deep:], depth) for v in (a, b, c))
    grad_input[...] = (
        inv * total[:, :depth] * gain[...] - x[...].astype(F32) * inv * inv * mean
    ).astype(BF)


def operands(group, refs):
    blocks, inv, gain = pairs(refs[4:-2]), refs[-2], refs[-1]
    inv = jnp.concatenate([inv[label(s)] for s in range(4)], axis=0)
    normed = (tokens(blocks, 0).astype(F32) * inv * gain[...]).astype(BF)
    return normed, tokens(blocks, 1)


def product(left, right):
    return lax.dot_general(left, right, CONTRACT_FIRST, preferred_element_type=F32)


def columns(messages, start, stop):
    return jnp.concatenate([m[:, start:stop] for m in messages], axis=0)


def early_grads(group, *refs):
    refs, outs = refs[:-3], refs[-3:]
    normed, grad = operands(group, refs)
    width = outs[0].shape[1]
    top = refs[0].shape[1]
    for at in (0, 1):
        outs[at][...] = product(normed, columns(refs[:4], at * width, at * width + width))
    outs[2][...] = product(columns(refs[:4], top - width, top), grad)


def wide_grads(at, group, *refs):
    refs, total, out = refs[:-2], refs[-2], refs[-1]
    normed, _ = operands(group, refs)
    width = out.shape[1]
    part = product(normed, columns(refs[:4], at * width, at * width + width))
    out[...] = (total[...] + part).astype(BF)


def down_grads(group, *refs):
    hidden, blocks, total, out = refs[:4], pairs(refs[4:-2]), refs[-2], refs[-1]
    part = product(jnp.concatenate([h[...] for h in hidden], axis=0), tokens(blocks, 1))
    out[...] = (total[...] + part).astype(BF)


def after(value, *earlier):
    return lax.optimization_barrier((value, *earlier))[0]


def shards(activations, out_grad, norm_gain, gate_w, up_w, down_w):
    rows, depth = activations.shape
    width = gate_w.shape[1]
    wide, deep = 3 * width + LANES, depth + LANES
    gain = norm_gain[None, :]

    gate_w, up_w, down_w = load([gate_w, up_w, down_w])
    both = jnp.stack([activations, out_grad])
    home = jnp.stack([both] + [send(both, "zl", -k) for k in (1, 2, 3)])
    own = [home] + [send(home, "y", s) for s in STEPS[1:]]
    own[1] = after(own[1], gate_w, up_w, down_w)
    other = [send(o, "core", 1) for o in own]

    def members(group):
        return [v for i in group for v in (own[i], other[i])]

    totals, crossed = [], []
    for group in GROUPS:
        tall = 32 * len(group)
        s0, s1, s2, s3 = call(
            lambda *a, n=len(group): forward(n, *a),
            [((tall, wide), F32)] + [((tall, wide), BF)] * 3,
            [*members(group), gain, gate_w, up_w, down_w],
        )
        total, out = call(
            add_x,
            [((tall, wide), F32), ((tall, wide), BF)],
            [s0, send(s1, "x", 1), send(s2, "x", 2), send(s3, "x", -1)],
        )
        totals.append(total)
        crossed.append(send(out, "zh", 1))

    messages, invs, halves = [], [], []
    gains = jnp.zeros((1, depth), F32)
    for group, total, arrived in zip(GROUPS, totals, crossed):
        size = len(group)
        tall = 32 * size
        if len(invs) < len(GROUPS) - 1:
            shapes = [((tall, wide), BF)]
        else:
            shapes = [((tall, 2 * width + LANES), BF), ((tall, width), BF)]
        m0, *hidden = call(activate, shapes, [total, arrived])
        found = [m0, send(m0, "x", -1), send(m0, "x", 2), send(m0, "x", 1)]
        mine, theirs, inv, gains = call(
            lambda *a, n=size: backward(n, *a),
            [((64 * size, deep), F32), ((64 * size + 8, deep), F32), ((4, tall, 1), F32)]
            + [((1, depth), F32)],
            [*found, *members(group), gate_w, up_w, gains],
        )
        received = send(theirs, "core", 1)
        halves.append((mine, received))
        if not messages:
            early = call(
                lambda *a: early_grads(group, *a),
                [((depth, width), F32)] * 2 + [((width, depth), F32)],
                [*found, *members(group), inv, gain],
                limit=32,
            )
            gains = after(gains, *early)
        messages += found
        invs.append(inv)

    parts = call(
        add_core,
        [((64, deep + LANES), BF)] * 4,
        [*[h[0] for h in halves], *[h[1] for h in halves], gains],
    )
    parts = [parts[0]] + [send(parts[i], "y", -STEPS[i]) for i in (1, 2, 3)]
    gain_sum, *outs = call(
        add_y,
        [((1, depth), F32), ((16, deep), F32)] + [((16, deep + 2 * LANES), BF)] * 3,
        parts,
    )
    hidden = after(hidden[0], *found[1:])
    units = [hidden] + [send(hidden, "x", s) for s in (-1, 2, 1)]
    (grad_down,) = call(
        lambda *a: down_grads(group, *a),
        [((width, depth), BF)],
        [*units, *members(group), early[2]],
        limit=32,
    )
    grad_gate, grad_up = (
        call(
            lambda *a, n=at: wide_grads(n, group, *a),
            [((depth, width), BF)],
            [*found, *members(group), inv, gain, early[at]],
            limit=32,
        )[0]
        for at in (0, 1)
    )
    home_sums = [outs[0]]
    home_sums += [send(after(outs[k], grad_up, grad_gate), "zl", k) for k in (1, 2, 3)]
    grad_input, grad_gain = call(
        finish,
        [((rows, depth), BF), ((1, depth), F32)],
        [*home_sums, gain_sum, activations, invs[0], gain],
    )
    return (grad_input, grad_gain[0], grad_gate, grad_up, grad_down)


def solution(mesh):
    fine = Mesh(mesh.devices.reshape(4, 2, 4, 4, 2), AXES)
    row, col = ("x", "zh"), ("y", "zl", "core")
    in_specs = (P(col, row), P(col, row), P(row), P(row, col), P(row, col), P(col, row))
    out_specs = (P(col, row), P(row), P(row, col), P(row, col), P(col, row))
    return jax.shard_map(shards, mesh=fine, in_specs=in_specs, out_specs=out_specs, check_vma=False)
```

```python
import jax
import jax.numpy as jnp
from jax import lax
from jax.experimental import pallas as pl
from jax.experimental.pallas import tpu as pltpu
from jax.sharding import Mesh
from jax.sharding import PartitionSpec as P

D = 8192
FF = 28672
BF = jnp.bfloat16
F32 = jnp.float32
LANES = 128
AXES = ("x", "zh", "y", "zl", "core")
CONTRACT_LAST = (((1,), (1,)), ((), ()))
CONTRACT_FIRST = (((0,), (0,)), ((), ()))
STEPS = (0, 1, -1, 2)
PARTS = 4
GROUPS = ((0, 1), (2, 3))
END = 16
WIDTH = FF // 32
GAINS = GROUPS[-1]


def ring(size, step):
    return [(i, (i + step) % size) for i in range(size)]


def send(value, axis, step):
    return lax.ppermute(value, axis, ring(2 if axis in ("zh", "core") else 4, step))


def tail(*columns):
    lane = lax.broadcasted_iota(jnp.int32, (columns[0].shape[0], LANES), 1)
    out = jnp.zeros((columns[0].shape[0], LANES), F32)
    at = 0
    for rest in columns:
        for _ in range(3):
            piece = rest.astype(BF).astype(F32)
            out = jnp.where(lane == at, piece, out)
            rest = rest - piece
            at += 1
    return out


def spots(rows):
    line = lax.broadcasted_iota(jnp.int32, (rows, LANES), 0)
    return line == lax.broadcasted_iota(jnp.int32, (rows, LANES), 1)


def lay(*columns):
    line = lax.broadcasted_iota(jnp.int32, (END, LANES), 0)
    out, at = jnp.zeros((END, LANES), F32), 0
    for column in columns:
        rest = jnp.sum(jnp.where(spots(column.shape[0]), column, 0.0), axis=0, keepdims=True)
        for _ in range(3):
            piece = rest.astype(BF).astype(F32)
            out = jnp.where(line == at, piece, out)
            rest = rest - piece
            at += 1
    return out


def stand(block, at, rows):
    row = block[at : at + 1] + block[at + 1 : at + 2] + block[at + 2 : at + 3]
    return jnp.sum(jnp.where(spots(rows), row, 0.0), axis=1, keepdims=True)


def tiles(ref, start, width, rows):
    return jnp.concatenate(
        [ref[start + j * rows : start + j * rows + rows] for j in range(width // LANES)], axis=1
    )


def head(block, at):
    return block[:, at : at + 1] + block[:, at + 1 : at + 2] + block[:, at + 2 : at + 3]


def call(kernel, out_shapes, args, limit=24):
    return pl.pallas_call(
        kernel,
        out_shape=[jax.ShapeDtypeStruct(s, d) for s, d in out_shapes],
        compiler_params=pltpu.CompilerParams(vmem_limit_bytes=limit * 1024 * 1024),
    )(*args)


def load(weights):
    count = len(weights)

    def kernel(*refs):
        sems, copies = refs[-1], []
        for n, (source, target) in enumerate(zip(refs[:count], refs[count : 2 * count])):
            step = source.shape[0] // PARTS
            for p in range(PARTS):
                rows = pl.ds(p * step, step)
                copies.append(
                    pltpu.make_async_copy(source.at[rows], target.at[rows], sems.at[n, p])
                )
        for copy in copies:
            copy.start()
        for copy in copies:
            copy.wait()

    return pl.pallas_call(
        kernel,
        out_shape=[jax.ShapeDtypeStruct(w.shape, w.dtype) for w in weights],
        in_specs=[pl.BlockSpec(memory_space=pltpu.HBM)] * count,
        out_specs=[pl.BlockSpec(memory_space=pltpu.VMEM)] * count,
        scratch_shapes=[pltpu.SemaphoreType.DMA((count, PARTS))],
        compiler_params=pltpu.CompilerParams(vmem_limit_bytes=24 * 1024 * 1024),
    )(*[pltpu.with_memory_space_constraint(w, pltpu.HBM) for w in weights])


def pack(row, rows):
    pieces = []
    for _ in range(3):
        pieces.append(row.astype(BF).astype(F32))
        row = row - pieces[-1]
    cuts = row.shape[1] // LANES
    line = lax.broadcasted_iota(jnp.int32, (rows, LANES), 0)
    tiles = [jnp.zeros((rows, LANES), F32) for _ in range(-(-3 * cuts // rows))]
    for at in range(3 * cuts):
        piece = pieces[at // cuts][:, at % cuts * LANES : at % cuts * LANES + LANES]
        tiles[at // rows] = jnp.where(line == at % rows, piece, tiles[at // rows])
    return jnp.concatenate(tiles, axis=1).astype(BF)


def unpack(block, width):
    block, rows, cuts = block.astype(F32), block.shape[0], width // LANES
    cut = [
        block[at % rows : at % rows + 1, at // rows * LANES : at // rows * LANES + LANES]
        for at in range(3 * cuts)
    ]
    return sum(jnp.concatenate(cut[p * cuts : p * cuts + cuts], axis=1) for p in range(3))


def label(slot):
    return lax.rem(lax.axis_index("x") + slot, 4)


def tokens(blocks, which):
    at = [label(s) for s in range(4)]
    return jnp.concatenate(
        [ref[at[s], which] for s in range(4) for pair in blocks for ref in pair], axis=0
    )


def pairs(refs):
    return [(refs[i], refs[i + 1]) for i in range(0, len(refs), 2)]


def forward(size, *refs):
    blocks, (gain, gate_w, up_w, down_w, *outs) = pairs(refs[: 2 * size]), refs[2 * size :]
    x = tokens(blocks, 0).astype(F32)
    scaled = (x * gain[...]).astype(BF)
    grad = tokens(blocks, 1)
    rows, width = 32 * size, gate_w.shape[1]

    cuts = width // LANES

    def put(value, start):
        for s in range(4):
            for j in range(cuts):
                part = value[rows * s : rows * s + rows, j * LANES : j * LANES + LANES]
                at = (start + j) * rows
                outs[s][at : at + rows] = part.astype(outs[s].dtype)

    put(jnp.dot(scaled, gate_w[...], preferred_element_type=F32), 0)
    put(jnp.dot(scaled, up_w[...], preferred_element_type=F32), cuts)
    put(
        lax.dot_general(grad, down_w[...], CONTRACT_LAST, preferred_element_type=F32),
        2 * cuts,
    )
    square = jnp.sum(x * x, axis=1, keepdims=True)
    for s in range(4):
        outs[s][3 * cuts * rows :] = lay(square[rows * s : rows * s + rows]).astype(outs[s].dtype)


def add_x(own, a, b, c, total, out):
    value = own[...] + a[...].astype(F32) + b[...].astype(F32) + c[...].astype(F32)
    end = lay(stand(value[-END:], 0, LANES))
    total[:-END], total[-END:] = value[:-END], end
    out[:-END], out[-END:] = value[:-END].astype(BF), end.astype(BF)


def activate(own, other, out, hidden=None):
    total = own[...] + other[...].astype(F32)
    size = (total.shape[0] - END) // 3
    rows = size * LANES // WIDTH
    inv = lax.rsqrt(stand(total[-END:], 0, rows) / D + 1e-05)
    every = jnp.concatenate([inv] * (size // rows), axis=0)
    gate = total[:size] * every
    up = total[size : 2 * size] * every
    back = total[2 * size : 3 * size]
    sig = 1.0 / (1.0 + jnp.exp(-gate))
    silu = gate * sig
    d_gate = back * up * sig * (1.0 + gate * (1.0 - sig))
    d_up = back * silu
    terms = d_gate * gate + d_up * up
    mean = jnp.sum(
        sum(terms[at : at + rows] for at in range(0, size, rows)), axis=1, keepdims=True
    )
    out[:size] = d_gate.astype(BF)
    out[size : 2 * size] = d_up.astype(BF)
    out[2 * size : 2 * size + END] = lay(inv, mean).astype(BF)
    if hidden is None:
        out[2 * size + END :] = (silu * up).astype(BF)
    else:
        hidden[...] = (silu * up).astype(BF)


def backward(size, *refs):
    messages, blocks = refs[:4], pairs(refs[4 : 4 + 2 * size])
    gate_w, up_w, last_gain, mine, theirs, inv_out, gain_out = refs[4 + 2 * size :]
    rows, (depth, width) = 32 * size, gate_w.shape

    size_of = rows * width // LANES

    def rows_of(at):
        return jnp.concatenate([tiles(m, at * size_of, width, rows) for m in messages], axis=0)

    part = lax.dot_general(
        rows_of(0), gate_w[...], CONTRACT_LAST, preferred_element_type=F32
    ) + lax.dot_general(rows_of(1), up_w[...], CONTRACT_LAST, preferred_element_type=F32)
    ends = [m[2 * size_of : 2 * size_of + END].astype(F32) for m in messages]
    inv = jnp.concatenate([stand(e, 0, rows) for e in ends], axis=0)
    mean = tail(jnp.concatenate([stand(e, 3, rows) for e in ends], axis=0))
    x = tokens(blocks, 0).astype(F32)
    gain = last_gain[...] + jnp.sum(part * x * inv, axis=0, keepdims=True)
    for s in range(4):
        at = label(s)
        inv_out[at] = inv[rows * s : rows * s + rows]
        for i in range(size):
            place = pl.ds(pl.multiple_of(64 * i + 16 * at, 16), 16)
            for core, out in enumerate((mine, theirs)):
                start = rows * s + 32 * i + 16 * core
                out[place, :depth] = part[start : start + 16].astype(out.dtype)
                out[place, depth:] = mean[start : start + 16].astype(out.dtype)
    gain_out[...] = gain
    packed = pack(gain, END)
    theirs[64 * size :, : packed.shape[1]] = packed
    theirs[64 * size :, packed.shape[1] :] = jnp.zeros((END, depth + LANES - packed.shape[1]), BF)


def add_core(*refs):
    count = len(GROUPS)
    mine, received, gains, outs = refs[:count], refs[count : 2 * count], refs[-5], refs[-4:]
    depth = gains.shape[1]
    last = 64 * len(GROUPS[-1])
    packed = pack(gains[...] + unpack(received[-1][last : last + END, : 2 * LANES], depth), 64)
    for g, group in enumerate(GROUPS):
        for i, block in enumerate(group):
            rows = slice(64 * i, 64 * i + 64)
            value, out = mine[g][rows] + received[g][rows].astype(F32), outs[block]
            out[:, :depth] = value[:, :depth].astype(BF)
            out[:, depth : depth + LANES] = tail(head(value[:, depth:], 0)).astype(BF)
            out[:, depth + LANES :] = packed


def add_y(*refs):
    parts, gain_out, outs = refs[:4], refs[4], refs[5:]
    depth = gain_out.shape[1]
    deep = depth + LANES
    total = sum(p[:, :deep].astype(F32) for p in parts)
    gain = sum(unpack(p[:, deep:], depth) for p in parts)
    gain_out[...] = gain
    outs[0][...] = total[:16]
    packed = pack(gain, 16)
    for s in range(1, 4):
        outs[s][:, :depth] = total[16 * s : 16 * s + 16, :depth].astype(BF)
        outs[s][:, depth:deep] = tail(head(total[16 * s : 16 * s + 16, depth:], 0)).astype(BF)
        outs[s][:, deep:] = packed


def finish(own, a, b, c, own_gain, x, inv, gain, grad_input, grad_gain):
    depth = x.shape[1]
    deep = depth + LANES
    total = own[...] + sum(v[:, :deep].astype(F32) for v in (a, b, c))
    inv = inv[0, :16]
    mean = head(total[:, depth:], 0) / D
    grad_gain[...] = own_gain[...] + sum(unpack(v[:, deep:], depth) for v in (a, b, c))
    grad_input[...] = (
        inv * total[:, :depth] * gain[...] - x[...].astype(F32) * inv * inv * mean
    ).astype(BF)


def operands(group, refs):
    blocks, inv, gain = pairs(refs[4:-2]), refs[-2], refs[-1]
    inv = jnp.concatenate([inv[label(s)] for s in range(4)], axis=0)
    normed = (tokens(blocks, 0).astype(F32) * inv * gain[...]).astype(BF)
    return normed, tokens(blocks, 1)


def product(left, right):
    return lax.dot_general(left, right, CONTRACT_FIRST, preferred_element_type=F32)


def columns(messages, start, width, rows):
    return jnp.concatenate([tiles(m, start, width, rows) for m in messages], axis=0)


def early_grads(group, *refs):
    refs, outs = refs[:-3], refs[-3:]
    normed, grad = operands(group, refs)
    width, rows = outs[0].shape[1], 32 * len(group)
    size = rows * width // LANES
    for at in (0, 1):
        outs[at][...] = product(normed, columns(refs[:4], at * size, width, rows))
    outs[2][...] = product(columns(refs[:4], 2 * size + END, width, rows), grad)


def wide_grads(at, group, *refs):
    refs, total, out = refs[:-2], refs[-2], refs[-1]
    normed, _ = operands(group, refs)
    width, rows = out.shape[1], 32 * len(group)
    start = at * rows * width // LANES
    part = product(normed, columns(refs[:4], start, width, rows))
    out[...] = (total[...] + part).astype(BF)


def down_grads(group, *refs):
    hidden, blocks, total, out = refs[:4], pairs(refs[4:-2]), refs[-2], refs[-1]
    part = product(columns(hidden, 0, out.shape[0], 32 * len(group)), tokens(blocks, 1))
    out[...] = (total[...] + part).astype(BF)


def after(value, *earlier):
    return lax.optimization_barrier((value, *earlier))[0]


def shards(activations, out_grad, norm_gain, gate_w, up_w, down_w):
    rows, depth = activations.shape
    width = gate_w.shape[1]
    deep = depth + LANES
    gain = norm_gain[None, :]

    gate_w, up_w, down_w = load([gate_w, up_w, down_w])
    both = jnp.stack([activations, out_grad])
    home = jnp.stack([both] + [send(both, "zl", -k) for k in (1, 2, 3)])
    own = [home] + [send(home, "y", s) for s in STEPS[1:]]
    own[1] = after(own[1], gate_w, up_w, down_w)
    other = [send(o, "core", 1) for o in own]

    def members(group):
        return [v for i in group for v in (own[i], other[i])]

    totals, crossed = [], []
    for group in GROUPS:
        size = 32 * len(group) * width // LANES
        s0, s1, s2, s3 = call(
            lambda *a, n=len(group): forward(n, *a),
            [((3 * size + END, LANES), F32)] + [((3 * size + END, LANES), BF)] * 3,
            [*members(group), gain, gate_w, up_w, down_w],
        )
        total, out = call(
            add_x,
            [((3 * size + END, LANES), F32), ((3 * size + END, LANES), BF)],
            [s0, send(s1, "x", 1), send(s2, "x", 2), send(s3, "x", -1)],
        )
        totals.append(total)
        crossed.append(send(out, "zh", 1))

    messages, invs, halves = [], [], []
    gains = jnp.zeros((1, depth), F32)
    for group, total, arrived in zip(GROUPS, totals, crossed):
        size = len(group)
        tall = 32 * size
        cut = tall * width // LANES
        if len(invs) < len(GROUPS) - 1:
            shapes = [((3 * cut + END, LANES), BF)]
        else:
            shapes = [((2 * cut + END, LANES), BF), ((cut, LANES), BF)]
        m0, *hidden = call(activate, shapes, [total, arrived])
        found = [m0, send(m0, "x", -1), send(m0, "x", 2), send(m0, "x", 1)]
        mine, theirs, inv, gains = call(
            lambda *a, n=size: backward(n, *a),
            [((64 * size, deep), F32), ((64 * size + END, deep), BF), ((4, tall, 1), F32)]
            + [((1, depth), F32)],
            [*found, *members(group), gate_w, up_w, gains],
        )
        received = send(theirs, "core", 1)
        halves.append((mine, received))
        if not messages:
            early = call(
                lambda *a: early_grads(group, *a),
                [((depth, width), F32)] * 2 + [((width, depth), F32)],
                [*found, *members(group), inv, gain],
                limit=32,
            )
            gains = after(gains, *early)
        messages += found
        invs.append(inv)

    parts = call(
        add_core,
        [((64, deep + LANES), BF)] * 4,
        [*[h[0] for h in halves], *[h[1] for h in halves], gains],
    )
    parts = [parts[0]] + [send(parts[i], "y", -STEPS[i]) for i in (1, 2, 3)]
    gain_sum, *outs = call(
        add_y,
        [((1, depth), F32), ((16, deep), F32)] + [((16, deep + 2 * LANES), BF)] * 3,
        parts,
    )
    hidden = after(hidden[0], *found[1:])
    units = [hidden] + [send(hidden, "x", s) for s in (-1, 2, 1)]
    (grad_down,) = call(
        lambda *a: down_grads(group, *a),
        [((width, depth), BF)],
        [*units, *members(group), early[2]],
        limit=32,
    )
    grad_gate, grad_up = (
        call(
            lambda *a, n=at: wide_grads(n, group, *a),
            [((depth, width), BF)],
            [*found, *members(group), inv, gain, early[at]],
            limit=32,
        )[0]
        for at in (0, 1)
    )
    home_sums = [outs[0]]
    home_sums += [send(after(outs[k], grad_up, grad_gate), "zl", k) for k in (1, 2, 3)]
    grad_input, grad_gain = call(
        finish,
        [((rows, depth), BF), ((1, depth), F32)],
        [*home_sums, gain_sum, activations, invs[0], gain],
    )
    return (grad_input, grad_gain[0], grad_gate, grad_up, grad_down)


def solution(mesh):
    fine = Mesh(mesh.devices.reshape(4, 2, 4, 4, 2), AXES)
    row, col = ("x", "zh"), ("y", "zl", "core")
    in_specs = (P(col, row), P(col, row), P(row), P(row, col), P(row, col), P(col, row))
    out_specs = (P(col, row), P(row), P(row, col), P(row, col), P(col, row))
    return jax.shard_map(shards, mesh=fine, in_specs=in_specs, out_specs=out_specs, check_vma=False)
```

```python
import jax
import jax.numpy as jnp
from jax import lax
from jax.experimental import pallas as pl
from jax.experimental.pallas import tpu as pltpu
from jax.sharding import Mesh
from jax.sharding import PartitionSpec as P

D = 8192
FF = 28672
BF = jnp.bfloat16
F32 = jnp.float32
LANES = 128
AXES = ("x", "zh", "y", "zl", "core")
CONTRACT_LAST = (((1,), (1,)), ((), ()))
CONTRACT_FIRST = (((0,), (0,)), ((), ()))
STEPS = (0, 1, -1, 2)
PARTS = 4
GROUPS = ((0, 1), (2, 3))
END = 16
WIDTH = FF // 32
GAINS = GROUPS[-1]


def ring(size, step):
    return [(i, (i + step) % size) for i in range(size)]


def send(value, axis, step):
    return lax.ppermute(value, axis, ring(2 if axis in ("zh", "core") else 4, step))


def tail(*columns):
    lane = lax.broadcasted_iota(jnp.int32, (columns[0].shape[0], LANES), 1)
    out = jnp.zeros((columns[0].shape[0], LANES), F32)
    at = 0
    for rest in columns:
        for _ in range(3):
            piece = rest.astype(BF).astype(F32)
            out = jnp.where(lane == at, piece, out)
            rest = rest - piece
            at += 1
    return out


def spots(rows):
    line = lax.broadcasted_iota(jnp.int32, (rows, LANES), 0)
    return line == lax.broadcasted_iota(jnp.int32, (rows, LANES), 1)


def lay(*columns):
    line = lax.broadcasted_iota(jnp.int32, (END, LANES), 0)
    out, at = jnp.zeros((END, LANES), F32), 0
    for column in columns:
        rest = jnp.sum(jnp.where(spots(column.shape[0]), column, 0.0), axis=0, keepdims=True)
        for _ in range(3):
            piece = rest.astype(BF).astype(F32)
            out = jnp.where(line == at, piece, out)
            rest = rest - piece
            at += 1
    return out


def stand(block, at, rows):
    row = block[at : at + 1] + block[at + 1 : at + 2] + block[at + 2 : at + 3]
    return jnp.sum(jnp.where(spots(rows), row, 0.0), axis=1, keepdims=True)


def tiles(ref, start, width, rows):
    return jnp.concatenate(
        [ref[start + j * rows : start + j * rows + rows] for j in range(width // LANES)], axis=1
    )


def head(block, at):
    return block[:, at : at + 1] + block[:, at + 1 : at + 2] + block[:, at + 2 : at + 3]


def call(kernel, out_shapes, args, limit=24):
    return pl.pallas_call(
        kernel,
        out_shape=[jax.ShapeDtypeStruct(s, d) for s, d in out_shapes],
        compiler_params=pltpu.CompilerParams(vmem_limit_bytes=limit * 1024 * 1024),
    )(*args)


def load(weights):
    count = len(weights)

    def kernel(*refs):
        sems, copies = refs[-1], []
        for n, (source, target) in enumerate(zip(refs[:count], refs[count : 2 * count])):
            step = source.shape[0] // PARTS
            for p in range(PARTS):
                rows = pl.ds(p * step, step)
                copies.append(
                    pltpu.make_async_copy(source.at[rows], target.at[rows], sems.at[n, p])
                )
        for copy in copies:
            copy.start()
        for copy in copies:
            copy.wait()

    return pl.pallas_call(
        kernel,
        out_shape=[jax.ShapeDtypeStruct(w.shape, w.dtype) for w in weights],
        in_specs=[pl.BlockSpec(memory_space=pltpu.HBM)] * count,
        out_specs=[pl.BlockSpec(memory_space=pltpu.VMEM)] * count,
        scratch_shapes=[pltpu.SemaphoreType.DMA((count, PARTS))],
        compiler_params=pltpu.CompilerParams(vmem_limit_bytes=24 * 1024 * 1024),
    )(*[pltpu.with_memory_space_constraint(w, pltpu.HBM) for w in weights])


def pack(row, rows):
    pieces = []
    for _ in range(3):
        pieces.append(row.astype(BF).astype(F32))
        row = row - pieces[-1]
    cuts = row.shape[1] // LANES
    line = lax.broadcasted_iota(jnp.int32, (rows, LANES), 0)
    tiles = [jnp.zeros((rows, LANES), F32) for _ in range(-(-3 * cuts // rows))]
    for at in range(3 * cuts):
        piece = pieces[at // cuts][:, at % cuts * LANES : at % cuts * LANES + LANES]
        tiles[at // rows] = jnp.where(line == at % rows, piece, tiles[at // rows])
    return jnp.concatenate(tiles, axis=1).astype(BF)


def unpack(block, width):
    block, rows, cuts = block.astype(F32), block.shape[0], width // LANES
    cut = [
        block[at % rows : at % rows + 1, at // rows * LANES : at // rows * LANES + LANES]
        for at in range(3 * cuts)
    ]
    return sum(jnp.concatenate(cut[p * cuts : p * cuts + cuts], axis=1) for p in range(3))


def label(slot):
    return lax.rem(lax.axis_index("x") + slot, 4)


def tokens(blocks, which):
    at = [label(s) for s in range(4)]
    return jnp.concatenate(
        [ref[at[s], which] for s in range(4) for pair in blocks for ref in pair], axis=0
    )


def pairs(refs):
    return [(refs[i], refs[i + 1]) for i in range(0, len(refs), 2)]


def forward(size, *refs):
    blocks, (gain, gate_w, up_w, down_w, *outs) = pairs(refs[: 2 * size]), refs[2 * size :]
    x = tokens(blocks, 0).astype(F32)
    scaled = (x * gain[...]).astype(BF)
    grad = tokens(blocks, 1)
    rows, width = 32 * size, gate_w.shape[1]

    cuts = width // LANES

    def put(value, start):
        for s in range(4):
            for j in range(cuts):
                part = value[rows * s : rows * s + rows, j * LANES : j * LANES + LANES]
                at = (start + j) * rows
                outs[s][at : at + rows] = part.astype(outs[s].dtype)

    put(jnp.dot(scaled, gate_w[...], preferred_element_type=F32), 0)
    put(jnp.dot(scaled, up_w[...], preferred_element_type=F32), cuts)
    put(
        lax.dot_general(grad, down_w[...], CONTRACT_LAST, preferred_element_type=F32),
        2 * cuts,
    )
    square = jnp.sum(x * x, axis=1, keepdims=True)
    for s in range(4):
        outs[s][3 * cuts * rows :] = lay(square[rows * s : rows * s + rows]).astype(outs[s].dtype)


def add_x(own, a, b, c, total, out):
    value = own[...] + a[...].astype(F32) + b[...].astype(F32) + c[...].astype(F32)
    end = lay(stand(value[-END:], 0, LANES))
    total[:-END], total[-END:] = value[:-END], end
    out[:-END], out[-END:] = value[:-END].astype(BF), end.astype(BF)


def activate(own, other, out, hidden=None):
    total = own[...] + other[...].astype(F32)
    size = (total.shape[0] - END) // 3
    rows = size * LANES // WIDTH
    inv = lax.rsqrt(stand(total[-END:], 0, rows) / D + 1e-05)
    every = jnp.concatenate([inv] * (size // rows), axis=0)
    gate = total[:size] * every
    up = total[size : 2 * size] * every
    back = total[2 * size : 3 * size]
    sig = 1.0 / (1.0 + jnp.exp(-gate))
    silu = gate * sig
    d_gate = back * up * sig * (1.0 + gate * (1.0 - sig))
    d_up = back * silu
    terms = d_gate * gate + d_up * up
    mean = jnp.sum(
        sum(terms[at : at + rows] for at in range(0, size, rows)), axis=1, keepdims=True
    )
    out[:size] = d_gate.astype(BF)
    out[size : 2 * size] = d_up.astype(BF)
    out[2 * size : 2 * size + END] = lay(inv, mean).astype(BF)
    if hidden is None:
        out[2 * size + END :] = (silu * up).astype(BF)
    else:
        hidden[...] = (silu * up).astype(BF)


def backward(size, *refs):
    messages, blocks = refs[:4], pairs(refs[4 : 4 + 2 * size])
    gate_w, up_w, last_gain, mine, theirs, inv_out, gain_out = refs[4 + 2 * size :]
    rows, (depth, width) = 32 * size, gate_w.shape

    size_of = rows * width // LANES

    def rows_of(at):
        return jnp.concatenate([tiles(m, at * size_of, width, rows) for m in messages], axis=0)

    part = lax.dot_general(
        rows_of(0), gate_w[...], CONTRACT_LAST, preferred_element_type=F32
    ) + lax.dot_general(rows_of(1), up_w[...], CONTRACT_LAST, preferred_element_type=F32)
    ends = [m[2 * size_of : 2 * size_of + END].astype(F32) for m in messages]
    inv = jnp.concatenate([stand(e, 0, rows) for e in ends], axis=0)
    mean = tail(jnp.concatenate([stand(e, 3, rows) for e in ends], axis=0))
    x = tokens(blocks, 0).astype(F32)
    gain = last_gain[...] + jnp.sum(part * x * inv, axis=0, keepdims=True)
    for s in range(4):
        at = label(s)
        inv_out[at] = inv[rows * s : rows * s + rows]
        for i in range(size):
            place = pl.ds(pl.multiple_of(64 * i + 16 * at, 16), 16)
            for core, out in enumerate((mine, theirs)):
                start = rows * s + 32 * i + 16 * core
                out[place, :depth] = part[start : start + 16].astype(out.dtype)
                out[place, depth:] = mean[start : start + 16].astype(out.dtype)
    gain_out[...] = gain
    packed = pack(gain, END)
    theirs[64 * size :, : packed.shape[1]] = packed
    theirs[64 * size :, packed.shape[1] :] = jnp.zeros((END, depth + LANES - packed.shape[1]), BF)


def add_core(*refs):
    count = len(GROUPS)
    mine, received, gains, outs = refs[:count], refs[count : 2 * count], refs[-5], refs[-4:]
    depth = gains.shape[1]
    last = 64 * len(GROUPS[-1])
    packed = pack(gains[...] + unpack(received[-1][last : last + END, : 2 * LANES], depth), 64)
    for g, group in enumerate(GROUPS):
        for i, block in enumerate(group):
            rows = slice(64 * i, 64 * i + 64)
            value, out = mine[g][rows] + received[g][rows].astype(F32), outs[block]
            out[:, :depth] = value[:, :depth].astype(BF)
            out[:, depth : depth + LANES] = tail(head(value[:, depth:], 0)).astype(BF)
            out[:, depth + LANES :] = packed


def add_y(*refs):
    parts, gain_out, outs = refs[:4], refs[4], refs[5:]
    depth = gain_out.shape[1]
    deep = depth + LANES
    total = sum(p[:, :deep].astype(F32) for p in parts)
    gain = sum(unpack(p[:, deep:], depth) for p in parts)
    gain_out[...] = gain
    outs[0][...] = total[:16]
    packed = pack(gain, 16)
    for s in range(1, 4):
        outs[s][:, :depth] = total[16 * s : 16 * s + 16, :depth].astype(BF)
        outs[s][:, depth:deep] = tail(head(total[16 * s : 16 * s + 16, depth:], 0)).astype(BF)
        outs[s][:, deep:] = packed


def finish(own, a, b, c, own_gain, x, inv, gain, grad_input, grad_gain):
    depth = x.shape[1]
    deep = depth + LANES
    total = own[...] + sum(v[:, :deep].astype(F32) for v in (a, b, c))
    inv = inv[0, :16]
    mean = head(total[:, depth:], 0) / D
    grad_gain[...] = own_gain[...] + sum(unpack(v[:, deep:], depth) for v in (a, b, c))
    grad_input[...] = (
        inv * total[:, :depth] * gain[...] - x[...].astype(F32) * inv * inv * mean
    ).astype(BF)


def operands(group, refs):
    blocks, inv, gain = pairs(refs[4:-2]), refs[-2], refs[-1]
    inv = jnp.concatenate([inv[label(s)] for s in range(4)], axis=0)
    normed = (tokens(blocks, 0).astype(F32) * inv * gain[...]).astype(BF)
    return normed, tokens(blocks, 1)


def product(left, right):
    return lax.dot_general(left, right, CONTRACT_FIRST, preferred_element_type=F32)


def columns(messages, start, width, rows):
    return jnp.concatenate([tiles(m, start, width, rows) for m in messages], axis=0)


def early_grads(group, *refs):
    refs, outs = refs[:-3], refs[-3:]
    normed, grad = operands(group, refs)
    width, rows = outs[0].shape[1], 32 * len(group)
    size = rows * width // LANES
    for at in (0, 1):
        outs[at][...] = product(normed, columns(refs[:4], at * size, width, rows))
    outs[2][...] = product(columns(refs[:4], 2 * size + END, width, rows), grad)


def wide_grads(at, group, *refs):
    refs, total, out = refs[:-2], refs[-2], refs[-1]
    normed, _ = operands(group, refs)
    width, rows = out.shape[1], 32 * len(group)
    start = at * rows * width // LANES
    part = product(normed, columns(refs[:4], start, width, rows))
    out[...] = (total[...] + part).astype(BF)


def down_grads(group, *refs):
    hidden, blocks, total, out = refs[:4], pairs(refs[4:-2]), refs[-2], refs[-1]
    part = product(columns(hidden, 0, out.shape[0], 32 * len(group)), tokens(blocks, 1))
    out[...] = (total[...] + part).astype(BF)


def after(value, *earlier):
    return lax.optimization_barrier((value, *earlier))[0]


def shards(activations, out_grad, norm_gain, gate_w, up_w, down_w):
    rows, depth = activations.shape
    width = gate_w.shape[1]
    deep = depth + LANES
    gain = norm_gain[None, :]

    gate_w, up_w, down_w = load([gate_w, up_w, down_w])
    both = jnp.stack([activations, out_grad])
    home = jnp.stack([both] + [send(both, "zl", -k) for k in (1, 2, 3)])
    own = [home] + [send(home, "y", s) for s in STEPS[1:]]
    own[1] = after(own[1], gate_w, up_w, down_w)
    other = [send(o, "core", 1) for o in own]

    def members(group):
        return [v for i in group for v in (own[i], other[i])]

    totals, crossed = [], []
    for group in GROUPS:
        size = 32 * len(group) * width // LANES
        s0, s1, s2, s3 = call(
            lambda *a, n=len(group): forward(n, *a),
            [((3 * size + END, LANES), F32)] + [((3 * size + END, LANES), BF)] * 3,
            [*members(group), gain, gate_w, up_w, down_w],
        )
        total, out = call(
            add_x,
            [((3 * size + END, LANES), F32), ((3 * size + END, LANES), BF)],
            [s0, send(s2, "x", 2), send(s1, "x", 1), send(s3, "x", -1)],
        )
        totals.append(total)
        crossed.append(send(out, "zh", 1))

    messages, invs, halves = [], [], []
    gains = jnp.zeros((1, depth), F32)
    for group, total, arrived in zip(GROUPS, totals, crossed):
        size = len(group)
        tall = 32 * size
        cut = tall * width // LANES
        if len(invs) < len(GROUPS) - 1:
            shapes = [((3 * cut + END, LANES), BF)]
        else:
            shapes = [((2 * cut + END, LANES), BF), ((cut, LANES), BF)]
        m0, *hidden = call(activate, shapes, [total, arrived])
        across = send(m0, "x", 2)
        found = [m0, send(m0, "x", -1), across, send(m0, "x", 1)]
        mine, theirs, inv, gains = call(
            lambda *a, n=size: backward(n, *a),
            [((64 * size, deep), F32), ((64 * size + END, deep), BF), ((4, tall, 1), F32)]
            + [((1, depth), F32)],
            [*found, *members(group), gate_w, up_w, gains],
        )
        received = send(theirs, "core", 1)
        halves.append((mine, received))
        if not messages:
            early = call(
                lambda *a: early_grads(group, *a),
                [((depth, width), F32)] * 2 + [((width, depth), F32)],
                [*found, *members(group), inv, gain],
                limit=32,
            )
            gains = after(gains, *early)
        messages += found
        invs.append(inv)

    parts = call(
        add_core,
        [((64, deep + LANES), BF)] * 4,
        [*[h[0] for h in halves], *[h[1] for h in halves], gains],
    )
    sent = {i: send(parts[i], "y", -STEPS[i]) for i in (3, 1, 2)}
    parts = [parts[0], sent[1], sent[2], sent[3]]
    gain_sum, *outs = call(
        add_y,
        [((1, depth), F32), ((16, deep), F32)] + [((16, deep + 2 * LANES), BF)] * 3,
        parts,
    )
    hidden = after(hidden[0], *found[1:])
    units = [hidden] + [send(hidden, "x", s) for s in (-1, 2, 1)]
    (grad_down,) = call(
        lambda *a: down_grads(group, *a),
        [((width, depth), BF)],
        [*units, *members(group), early[2]],
        limit=32,
    )
    grad_gate, grad_up = (
        call(
            lambda *a, n=at: wide_grads(n, group, *a),
            [((depth, width), BF)],
            [*found, *members(group), inv, gain, early[at]],
            limit=32,
        )[0]
        for at in (0, 1)
    )
    home_sums = [outs[0]]
    home_sums += [send(after(outs[k], grad_up, grad_gate), "zl", k) for k in (1, 2, 3)]
    grad_input, grad_gain = call(
        finish,
        [((rows, depth), BF), ((1, depth), F32)],
        [*home_sums, gain_sum, activations, invs[0], gain],
    )
    return (grad_input, grad_gain[0], grad_gate, grad_up, grad_down)


def solution(mesh):
    fine = Mesh(mesh.devices.reshape(4, 2, 4, 4, 2), AXES)
    row, col = ("x", "zh"), ("y", "zl", "core")
    in_specs = (P(col, row), P(col, row), P(row), P(row, col), P(row, col), P(col, row))
    out_specs = (P(col, row), P(row), P(row, col), P(row, col), P(col, row))
    return jax.shard_map(shards, mesh=fine, in_specs=in_specs, out_specs=out_specs, check_vma=False)
```
